32 devices in a mesh: region: 8 (over z, x), level: 4 (over y, core).
Axes of the slice: x: 2, y: 2, z: 4, core: 2. Of those that a mesh axis runs over, the one named last changes fastest.
Arguments:
- ensemble: bfloat16 [4, 256, 32768], P('level', None, 'region'), may hold values from -6 to 6
- obs_anomaly: bfloat16 [4, 8192, 256], P('level', 'region'), may hold values from -6 to 6
- innovation: bfloat16 [4, 8192], P('level', 'region'), may hold values from -18 to 18
- obs_precision: bfloat16 [4, 8192], P('level', 'region'), may hold values from 0.019897461 to 0.29882812
- owner_region: int32 [4, 8192, 1], P('level', 'region'), may hold values from 0 to 7; in each aligned block of 1024 rows (0 to 1023, 1024 to 2047, ..., all dimensions but the last counted through in order) at most 192 rows name the same one
- neighbours: int32 [8, 3], replicated, may hold values from 0 to 7, all different within a row
Outputs:
- analysis: bfloat16 [4, 256, 32768], P('level', None, 'region')
The draws below stay inside these ranges and needn't reach their ends.
Inputs may be any that keep to these rules, and one draw needn't show every extreme that they name: `owner_region`: among the 1024 observations of one device (aligned blocks), no region is named more than 192 times, a bound that some block reaches. `neighbours`: each row lists 3 different regions; every region is listed by some row.
All inputs are finite; a program needn't handle non-finite values.
Results may differ from the reference program's by a relative error of at most 0.0059.
Values may be sent and summed in bfloat16 or wider, within the bound.
A program may use at most 64 MiB of HBM per device.

```python
import math
import jax
import jax.numpy as jnp
import numpy as np
from jax import lax

MEMBERS = 256
NEIGH = 3
NSTEPS = 4
COL_DEV = 4096
OBS_DEV = 1024
REGIONS = 8
LEVELS = 4
CAP = 192
SLOTS = 768
COLS = 32768
OBS = 8192


def draw_obs_anomaly(key, part):
    pattern_key = jax.random.fold_in(key, 11)
    sign_key = jax.random.fold_in(key, 12)
    noise_key = jax.random.fold_in(key, 13)
    pattern = jnp.clip(jax.random.normal(pattern_key, (LEVELS, 1, MEMBERS), jnp.float32), -3.5, 3.5)
    flips = jax.random.bernoulli(sign_key, 0.5, (LEVELS, OBS, 1))
    signs = jnp.where(flips, 1.0, -1.0).astype(jnp.float32)
    noise = jax.random.normal(noise_key, (LEVELS, OBS, MEMBERS), jnp.float32)
    strength = 0.7
    values = strength * signs * pattern + noise
    return jnp.clip(values, -6.0, 6.0).astype(jnp.bfloat16)


def levels(rng, extent, cuts, smallest, top_value):
    def one(dim, blocks):
        draws = jax.random.uniform(jax.random.fold_in(jax.random.fold_in(rng, 6), dim), (blocks,), jnp.float32, smallest / len(cuts), top_value / len(cuts))
        return jnp.repeat(jnp.exp(draws), extent[dim] // blocks).reshape((-1,) + (1,) * (len(extent) - dim - 1))

    loudness = one(*cuts[0])
    for cut in cuts[1:]:
        loudness = loudness * one(*cut)
    return loudness


def picks_of(own_key, rows, count, top, lift):
    ranking = jax.random.permutation(jax.random.fold_in(own_key, 1), count)
    favour = ranking
    for power in range(3):
        favour = favour * favour // count
    favour = favour * lift // count
    tickets = jax.random.randint(jax.random.fold_in(own_key, 2), (rows, count), 0, 4096) + favour
    sure = jax.random.permutation(jax.random.fold_in(own_key, 3), rows)[jnp.arange(count) % rows]
    tickets = jnp.where(jnp.arange(rows)[:, None] == sure[None, :], 1 << 14, tickets)
    merit = tickets * count + jnp.arange(count)
    return lax.top_k(merit.astype(jnp.int32), top)[1].astype(jnp.int32)


def deal_out(stream_key, own, number, rows, count, top, bound, slope):
    sequence = jax.random.permutation(stream_key, count)
    packed, usual = load_shares(count, rows * top, bound, slope, True), load_shares(count, rows * top, bound, slope, False)
    places = jnp.arange(count)

    def named(sizes, rotation):
        used = int((sizes > 0).sum())
        fixed = max(1, used // 4)
        shifted = fixed + (places - fixed + rotation * (used - fixed)) % max(1, count - fixed)
        return jnp.zeros((count,), jnp.int32).at[sequence[jnp.where(places < fixed, places, shifted)]].set(jnp.asarray(sizes, jnp.int32))

    sizes = jnp.where(number % 4 == 0, named(packed, number // 4), named(usual, number - number // 4 - 1))
    mixed = jax.random.permutation(jax.random.fold_in(own, 3), count)
    giver, receiver = mixed[0:count // 2 * 2:2], mixed[1:count // 2 * 2:2]
    slack = jnp.minimum(sizes[giver] - 1, bound - sizes[receiver]) // 2
    slack = jnp.where((giver == sequence[0]) | (receiver == sequence[0]) | (sizes[receiver] == 0), 0, jnp.maximum(slack, 0))
    shifted = jax.random.randint(jax.random.fold_in(own, 4), (count // 2,), 0, 1 << 20) % (slack + 1)
    sizes = sizes.at[giver].add(-shifted).at[receiver].add(shifted)
    items = jnp.searchsorted(jnp.cumsum(sizes), jnp.arange(rows * top), side="right").astype(jnp.int32)
    listing = items.reshape(top, rows).T
    listing = listing[jax.random.permutation(jax.random.fold_in(own, 1), rows)]
    rotation = jax.random.randint(jax.random.fold_in(own, 2), (rows, 1), 0, top)
    return jnp.take_along_axis(listing, (jnp.arange(top)[None, :] + rotation) % top, axis=1)


def load_shares(count, total, most, slope, full):
    portions = [(1 << 20) // math.isqrt(grade ** slope) + 1 for grade in range(1, count + 1)]
    largest = most if full else min(most, max(-(-total // count), total * portions[0] // sum(portions)))
    least = 1 if total - largest >= count - 1 else 0
    counts, surplus = [largest] + [least] * (count - 1), total - largest - least * (count - 1)
    while surplus > 0:
        candidates = [i for i in range(1, count) if counts[i] < largest] or [i for i in range(1, count) if counts[i] < most]
        whole, left = sum([portions[i] for i in candidates]), surplus
        for i in candidates:
            extra = min(most - counts[i], max(1, left * portions[i] // whole), surplus)
            counts[i] = counts[i] + extra
            surplus = surplus - extra
    return np.array(counts)


def centred(stream_key, shape, deviation, reach, cuts=(), kind=jnp.bfloat16):
    entries = jax.random.normal(stream_key, shape, jnp.float32) * deviation
    if len(cuts) > 0:
        entries = levels(stream_key, shape, cuts, -0.22, 0.18) * entries
    return jnp.clip(entries, min=-reach, max=reach).astype(kind)


def setup_inputs(seed: int = 0) -> dict:
    seeds = jax.random.split(jax.random.key(seed), 7)
    ensemble = centred(seeds[0], (LEVELS, MEMBERS, COLS), 1.0, 6.0, ((0, 4), (2, 8)))
    obs_anomaly = draw_obs_anomaly(jax.random.fold_in(seeds[6], 71), 0)
    innovation = centred(seeds[2], (LEVELS, OBS), 3.0, 18.0, ((0, 4), (1, 8)))
    obs_precision = jnp.clip(jnp.exp(math.log(0.29882812) - 2.7092764 * jax.random.uniform(seeds[3], (LEVELS, OBS), jnp.float32) ** levels(seeds[3], (LEVELS, OBS), ((0, 4), (1, 8)), -0.2, 0.2)), 0.019897461, 0.29882812).astype(jnp.bfloat16)
    owner_region_keys = jax.random.split(jax.random.fold_in(seeds[4], 1), LEVELS * OBS // OBS_DEV)
    owner_region_turns = jax.random.permutation(jax.random.fold_in(seeds[4], 3), LEVELS * OBS // OBS_DEV)
    owner_region = jax.vmap(lambda own, number: deal_out(jax.random.fold_in(seeds[4], 2), own, number, OBS_DEV, REGIONS, 1, CAP, 2))(owner_region_keys, owner_region_turns).reshape((LEVELS, OBS, 1))
    neighbours = picks_of(seeds[5], REGIONS, REGIONS, NEIGH, 0)
    return dict(ensemble=ensemble, obs_anomaly=obs_anomaly, innovation=innovation, obs_precision=obs_precision, owner_region=owner_region, neighbours=neighbours)


TAPER = 0.6

def neighbour_weights(neighbours):
    region_ids = jnp.arange(neighbours.shape[0], dtype=jnp.int32)
    weights = (region_ids[:, None] == region_ids[None, :]).astype(jnp.float32)
    for listed in range(neighbours.shape[1]):
        hit = (neighbours[:, listed][:, None] == region_ids[None, :]).astype(jnp.float32)
        weights = weights + TAPER ** (listed + 1) * hit
    return weights

def inverse_root(matrix):
    order_size = matrix.shape[0]
    identity = jnp.eye(order_size, dtype=jnp.float32)
    norm_scale = 0.5 * jnp.sqrt(jnp.sum(matrix * matrix))
    root_iter = matrix / norm_scale
    inverse_iter = identity
    for newton_step in range(NSTEPS):
        correction = 1.5 * identity - 0.5 * jnp.dot(inverse_iter, root_iter, precision=lax.Precision.HIGHEST)
        root_iter = jnp.dot(root_iter, correction, precision=lax.Precision.HIGHEST)
        inverse_iter = jnp.dot(correction, inverse_iter, precision=lax.Precision.HIGHEST)
    return inverse_iter / jnp.sqrt(norm_scale)

def analysis_weights(covariance, innovation_sum):
    order_size = covariance.shape[0]
    identity = jnp.eye(order_size, dtype=jnp.float32)
    precision_matrix = covariance + (order_size - 1.0) * identity
    root = inverse_root(precision_matrix)
    inner = jnp.dot(root, innovation_sum, precision=lax.Precision.HIGHEST)
    mean_shift = jnp.dot(root, inner, precision=lax.Precision.HIGHEST)
    return (math.sqrt(order_size - 1.0) * root + mean_shift[:, None]).astype(jnp.bfloat16)

def update_columns(column_block, transform):
    average = lax.optimization_barrier(jnp.mean(column_block.astype(jnp.float32), axis=0))
    anomaly = (column_block.astype(jnp.float32) - average[None, :]).astype(jnp.bfloat16)
    combined = lax.dot_general(transform, anomaly, (((0,), (0,)), ((), ())), preferred_element_type=jnp.float32)
    return (combined + average[None, :]).astype(jnp.bfloat16)

def reference(ensemble, obs_anomaly, innovation, obs_precision, owner_region, neighbours):
    region_weight = neighbour_weights(neighbours)
    owner_ids = owner_region[:, :, 0]
    most_rows = REGIONS * SLOTS

    def one_region(region):
        weight_row = region_weight[region]
        level_covs = []
        level_sums = []
        for source in range(LEVELS):
            obs_weight = weight_row[owner_ids[source]]
            live = obs_weight > 0
            amount = jnp.sum(live.astype(jnp.int32))
            picked = jnp.nonzero(live, size=most_rows, fill_value=0)[0].astype(jnp.int32)
            valid = jnp.arange(most_rows, dtype=jnp.int32) < amount
            gain = (obs_weight[picked] * obs_precision[source][picked].astype(jnp.float32)).astype(jnp.bfloat16)
            gain = jnp.where(valid, gain, jnp.zeros_like(gain))
            picked_rows = obs_anomaly[source][picked]
            weighted = (gain.astype(jnp.float32)[:, None] * picked_rows.astype(jnp.float32)).astype(jnp.bfloat16)
            level_covs.append(jnp.dot(weighted.T, picked_rows, preferred_element_type=jnp.float32))
            level_sums.append(jnp.dot(innovation[source][picked], weighted, preferred_element_type=jnp.float32))
        results = []
        for target in range(LEVELS):
            covariance = jnp.zeros_like(level_covs[0])
            innovation_sum = jnp.zeros_like(level_sums[0])
            for source in range(LEVELS):
                factor = 0.5 ** abs(target - source)
                covariance = covariance + factor * level_covs[source]
                innovation_sum = innovation_sum + factor * level_sums[source]
            transform = analysis_weights(covariance, innovation_sum)
            column_block = lax.dynamic_slice_in_dim(ensemble[target], (region * COL_DEV).astype(jnp.int32), COL_DEV, 1)
            results.append(update_columns(column_block, transform))
        return jnp.stack(results)
    stacked = lax.map(one_region, jnp.arange(REGIONS, dtype=jnp.int32))
    members = ensemble.shape[1]
    return jnp.transpose(stacked, (1, 2, 0, 3)).reshape(LEVELS, members, REGIONS * COL_DEV)
```

```python
import functools
import math

import jax
import jax.numpy as jnp
from jax import lax
from jax.experimental import pallas as pl
from jax.experimental.pallas import tpu as pltpu
from jax.sharding import PartitionSpec as P

NSTEPS = 4
TAPER = 0.6
EXTRA = 16
F32 = jnp.float32
BF16 = jnp.bfloat16
MESH = pl.DeviceIdType.MESH


def each(count, step):
    if count <= 8:
        for k in range(count):
            step(k)
    else:
        lax.fori_loop(0, count, lambda k, c: (step(k), c)[1], 0)


def split(a):
    high = a.astype(BF16)
    return high, (a - high.astype(F32)).astype(BF16)


def dot(a, b):
    return jnp.dot(a, b, preferred_element_type=F32)


def product(a, b):
    return dot(a[0], b[0]) + (dot(a[0], b[1]) + dot(a[1], b[0]))


def weights_kernel(
    regions,
    levels,
    x_ref,
    owner_ref,
    prec_ref,
    innov_ref,
    neigh_ref,
    out_ref,
    gain,
    sums,
    xt,
    tx1,
    keep,
    rx1,
    tx2,
    rx2,
    tx3,
    rx3,
    mat,
    send1,
    recv1,
    send2,
    recv2,
    send3,
    recv3,
):
    groups = regions // 2
    members = x_ref.shape[1]
    half = members // 2
    me_r = lax.axis_index("region")
    me_l = lax.axis_index("level")
    my_group, side = lax.div(me_r, 2), lax.rem(me_r, 2)
    partner = my_group * 2 + (1 - side)

    def other_group(k):
        return lax.rem(my_group + 1 + k, groups)

    def other_level(k):
        return lax.rem(me_l + 1 + k, levels)

    barrier = pltpu.get_barrier_semaphore()

    def greet(region, level):
        pl.semaphore_signal(barrier, inc=1, device_id=(region, level), device_id_type=MESH)

    greet(partner, me_l)
    each(groups - 1, lambda k: greet(other_group(k) * 2 + side, me_l))
    each(levels - 1, lambda k: greet(me_r, other_level(k)))

    owner = owner_ref[...]
    ids = lax.broadcasted_iota(jnp.int32, (regions, owner.shape[1]), 0)
    weight = (ids == owner).astype(F32)
    for listed in range(neigh_ref.shape[1]):
        hit = (neigh_ref[:, listed : listed + 1] == owner).astype(F32)
        weight = weight + TAPER ** (listed + 1) * hit
    rounded = (weight * prec_ref[...].astype(F32)).astype(BF16).astype(F32)
    gain[...] = rounded
    sums[...] = dot((rounded * innov_ref[...].astype(F32)).astype(BF16), x_ref[...])
    xt[...] = x_ref[...].astype(F32).T

    row = lax.broadcasted_iota(jnp.int32, (half, half), 0)
    col = lax.broadcasted_iota(jnp.int32, (half, half), 1)
    line = lax.broadcasted_iota(jnp.int32, (EXTRA, half), 0)

    def contribution(region):
        weighted = (xt[...] * gain[pl.ds(region, 1), :]).astype(BF16)
        cov = dot(weighted, x_ref[...])
        low = cov[half:, half:]
        tri = jnp.where(row <= col, cov[:half, :half], low)
        diag = jnp.sum(jnp.where(row == col, low, 0.0), axis=0, keepdims=True)
        vec = sums[pl.ds(region, 1), :]
        extra = jnp.where(
            line == 0,
            diag,
            jnp.where(line == 1, vec[:, :half], jnp.where(line == 2, vec[:, half:], 0.0)),
        )
        return cov[:half, half:], tri, extra

    def store(ref, group, parts):
        kind = ref.dtype
        ref[group, 0:half, :] = parts[0].astype(kind)
        ref[group, half:members, :] = parts[1].astype(kind)
        ref[group, members : members + EXTRA, :] = parts[2].astype(kind)

    def copy1(group):
        return pltpu.make_async_remote_copy(
            src_ref=tx1.at[group],
            dst_ref=rx1.at[group],
            send_sem=send1.at[group],
            recv_sem=recv1.at[group],
            device_id=(partner, me_l),
            device_id_type=MESH,
        )

    def copy2(to, slot):
        return pltpu.make_async_remote_copy(
            src_ref=tx2.at[to],
            dst_ref=rx2.at[slot],
            send_sem=send2.at[to],
            recv_sem=recv2.at[slot],
            device_id=(to * 2 + side, me_l),
            device_id_type=MESH,
        )

    def copy3(to, slot):
        return pltpu.make_async_remote_copy(
            src_ref=tx3,
            dst_ref=rx3.at[slot],
            send_sem=send3.at[to],
            recv_sem=recv3.at[slot],
            device_id=(me_r, to),
            device_id_type=MESH,
        )

    store(tx1, other_group(0), contribution(other_group(0) * 2 + (1 - side)))
    pl.semaphore_wait(barrier, 1 + (groups - 1) + (levels - 1))
    copy1(other_group(0)).start()

    def give(k):
        group = other_group(k + 1)
        store(tx1, group, contribution(group * 2 + (1 - side)))
        copy1(group).start()

    each(groups - 1, give)

    def hold(k):
        group = other_group(k)
        store(keep, group, contribution(group * 2 + side))

    each(groups, hold)

    def fold(k):
        group = other_group(k)
        copy1(group).wait_recv()
        tx2[group] = (keep[group] + rx1[group].astype(F32)).astype(BF16)
        copy2(group, my_group).start()

    each(groups - 1, fold)
    copy1(my_group).wait_recv()
    keep[my_group] = keep[my_group] + rx1[my_group].astype(F32)

    def gather(k):
        group = other_group(k)
        copy2(group, group).wait_recv()
        keep[my_group] = keep[my_group] + rx2[group].astype(F32)

    each(groups - 1, gather)
    total = keep[my_group]
    tx3[...] = total.astype(BF16)
    each(levels - 1, lambda k: copy3(other_level(k), me_l).start())
    for k in range(levels - 1):
        level = other_level(k)
        apart = jnp.abs(level - me_l)
        factor = jnp.float32(0.0)
        for distance in range(1, levels):
            factor = jnp.where(apart == distance, jnp.float32(0.5**distance), factor)
        copy3(level, level).wait_recv()
        total = total + factor * rx3[level].astype(F32)

    corner = total[:half]
    tri = total[half:members]
    flip = tri.T
    shift = members - 1.0
    mat[0:half, half:members] = corner
    mat[half:members, 0:half] = corner.T
    mat[0:half, 0:half] = jnp.where(row <= col, tri, flip) + jnp.where(row == col, shift, 0.0)
    mat[half:members, half:members] = jnp.where(
        row == col,
        total[members : members + 1] + shift,
        jnp.where(row > col, tri, flip),
    )
    vector = jnp.concatenate(
        [total[members + 1 : members + 2], total[members + 2 : members + 3]], axis=1
    )
    matrix = mat[...]
    norm = 0.5 * jnp.sqrt(
        jnp.sum(jnp.sum(matrix * matrix, axis=0, keepdims=True), axis=1, keepdims=True)
    )
    eye = (
        lax.broadcasted_iota(jnp.int32, (members, members), 0)
        == lax.broadcasted_iota(jnp.int32, (members, members), 1)
    ).astype(F32)
    root_iter = matrix / norm
    correction = 1.5 * eye - 0.5 * root_iter
    inverse_iter = correction
    left, right = split(root_iter), split(correction)
    root_iter = product(left, right)
    inverse = right
    for step in range(1, NSTEPS):
        left = split(root_iter)
        correction = split(1.5 * eye - 0.5 * product(inverse, left))
        if step < NSTEPS - 1:
            root_iter = product(left, correction)
        inverse_iter = product(correction, inverse)
        inverse = split(inverse_iter)
    inner = product(split(jnp.broadcast_to(vector, (8, members))), inverse)
    mean_shift = product(split(inner), inverse)[0:1] / norm
    table = math.sqrt(members - 1.0) * (inverse_iter / jnp.sqrt(norm)) + mean_shift
    spare = (1.0 - jnp.sum(table, axis=1, keepdims=True)) * (1.0 / members)
    out_ref[...] = (table + spare).astype(BF16)

    each(groups, lambda k: copy1(other_group(k)).wait_send())
    each(groups - 1, lambda k: copy2(other_group(k), my_group).wait_send())
    each(levels - 1, lambda k: copy3(other_level(k), me_l).wait_send())


def update_kernel(table_ref, block_ref, out_ref):
    out_ref[...] = dot(table_ref[...], block_ref[...]).astype(BF16)


def body(ensemble, obs_anomaly, innovation, obs_precision, owner_region, neighbours):
    regions = lax.axis_size("region")
    levels = lax.axis_size("level")
    groups = regions // 2
    obs, members = obs_anomaly.shape[1:]
    rows, half = members + EXTRA, members // 2
    vmem = pl.BlockSpec(memory_space=pltpu.VMEM)
    dma = pltpu.SemaphoreType.DMA
    table = pl.pallas_call(
        functools.partial(weights_kernel, regions, levels),
        out_shape=jax.ShapeDtypeStruct((members, members), BF16),
        in_specs=[vmem] * 5,
        out_specs=vmem,
        scratch_shapes=[
            pltpu.VMEM((regions, obs), F32),
            pltpu.VMEM((regions, members), F32),
            pltpu.VMEM((members, obs), F32),
            pltpu.VMEM((groups, rows, half), BF16),
            pltpu.VMEM((groups, rows, half), F32),
            pltpu.VMEM((groups, rows, half), BF16),
            pltpu.VMEM((groups, rows, half), BF16),
            pltpu.VMEM((groups, rows, half), BF16),
            pltpu.VMEM((rows, half), BF16),
            pltpu.VMEM((levels, rows, half), BF16),
            pltpu.VMEM((members, members), F32),
            dma((groups,)),
            dma((groups,)),
            dma((groups,)),
            dma((groups,)),
            dma((levels,)),
            dma((levels,)),
        ],
        compiler_params=pltpu.CompilerParams(
            collective_id=0, has_side_effects=True, vmem_limit_bytes=36 * 2**20
        ),
    )(
        obs_anomaly[0],
        owner_region.reshape(1, obs),
        obs_precision,
        innovation,
        neighbours,
    )
    columns = ensemble.shape[2]
    width = 1024
    return pl.pallas_call(
        update_kernel,
        out_shape=jax.ShapeDtypeStruct(ensemble.shape, BF16),
        grid=(columns // width,),
        in_specs=[
            pl.BlockSpec((members, members), lambda i: (0, 0)),
            pl.BlockSpec((None, members, width), lambda i: (0, 0, i)),
        ],
        out_specs=pl.BlockSpec((None, members, width), lambda i: (0, 0, i)),
    )(table, ensemble)


def solution(mesh):
    return jax.shard_map(
        body,
        mesh=mesh,
        in_specs=(
            P("level", None, "region"),
            P("level", "region", None),
            P("level", "region"),
            P("level", "region"),
            P("level", "region", None),
            P(),
        ),
        out_specs=P("level", None, "region"),
        check_vma=False,
    )
```

```python
import functools
import math

import jax
import jax.numpy as jnp
from jax import lax
from jax.experimental import pallas as pl
from jax.experimental.pallas import tpu as pltpu
from jax.sharding import PartitionSpec as P

NSTEPS = 4
TAPER = 0.6
EXTRA = 16
F32 = jnp.float32
BF16 = jnp.bfloat16
MESH = pl.DeviceIdType.MESH


def each(count, step):
    if count <= 8:
        for k in range(count):
            step(k)
    else:
        lax.fori_loop(0, count, lambda k, c: (step(k), c)[1], 0)


def dot(a, b):
    return jnp.dot(a, b, preferred_element_type=F32)


def shifted(scale, rest):
    return scale, rest, rest.astype(BF16)


def product(a, b):
    return shifted(a[0] * b[0], a[0] * b[1] + b[0] * a[1] + dot(a[2], b[2]))


def correct(a):
    return shifted(1.5 - 0.5 * a[0], -0.5 * a[1])


def apply(a, vector):
    rows = jnp.broadcast_to(vector, (8, vector.shape[1]))
    high = rows.astype(BF16)
    low = (rows - high.astype(F32)).astype(BF16)
    return (a[0] * rows + (dot(high, a[2]) + dot(low, a[2])))[0:1]


def weights_kernel(
    regions,
    levels,
    x_hbm,
    owner_hbm,
    prec_hbm,
    innov_hbm,
    neigh_hbm,
    out_ref,
    x_ref,
    owner_ref,
    prec_ref,
    innov_ref,
    neigh_ref,
    load_sem,
    gain,
    sums,
    xt,
    tx1,
    keep,
    rx1,
    tx2,
    rx2,
    tx3,
    rx3,
    mat,
    send1,
    recv1,
    send2,
    recv2,
    send3,
    recv3,
):
    groups = regions // 2
    members = x_ref.shape[1]
    half = members // 2
    me_r = lax.axis_index("region")
    me_l = lax.axis_index("level")
    my_group, side = lax.div(me_r, 2), lax.rem(me_r, 2)
    partner = my_group * 2 + (1 - side)

    def other_group(k):
        return lax.rem(my_group + 1 + k, groups)

    def other_level(k):
        return lax.rem(me_l + 1 + k, levels)

    loads = [
        pltpu.make_async_copy(source, target, load_sem.at[n])
        for n, (source, target) in enumerate(
            (
                (neigh_hbm, neigh_ref),
                (owner_hbm, owner_ref),
                (prec_hbm, prec_ref),
                (innov_hbm, innov_ref),
                (x_hbm, x_ref),
            )
        )
    ]
    for load in loads:
        load.start()

    barrier = pltpu.get_barrier_semaphore()

    def greet(region, level):
        pl.semaphore_signal(barrier, inc=1, device_id=(region, level), device_id_type=MESH)

    greet(partner, me_l)
    each(groups - 1, lambda k: greet(other_group(k) * 2 + side, me_l))
    each(levels - 1, lambda k: greet(me_r, other_level(k)))

    for load in loads[:4]:
        load.wait()
    owner = owner_ref[...]
    unit = (
        lax.broadcasted_iota(jnp.int32, (regions, regions), 0)
        == lax.broadcasted_iota(jnp.int32, (regions, regions), 1)
    ).astype(F32)
    lists = lax.dot_general(
        unit.astype(BF16),
        neigh_ref[...].astype(F32).astype(BF16),
        (((1,), (1,)), ((), ())),
        preferred_element_type=F32,
    ).astype(jnp.int32)
    ids = lax.broadcasted_iota(jnp.int32, (regions, owner.shape[1]), 0)
    weight = (ids == owner).astype(F32)
    for listed in range(neigh_ref.shape[0]):
        hit = (lists[:, listed : listed + 1] == owner).astype(F32)
        weight = weight + TAPER ** (listed + 1) * hit
    rounded = (weight * prec_ref[...].astype(F32)).astype(BF16).astype(F32)
    gain[...] = rounded
    loads[4].wait()
    sums[...] = dot((rounded * innov_ref[...].astype(F32)).astype(BF16), x_ref[...])
    xt[...] = x_ref[...].astype(F32).T

    row = lax.broadcasted_iota(jnp.int32, (half, half), 0)
    col = lax.broadcasted_iota(jnp.int32, (half, half), 1)
    line = lax.broadcasted_iota(jnp.int32, (EXTRA, half), 0)

    def contribution(region):
        weighted = (xt[...] * gain[pl.ds(region, 1), :]).astype(BF16)
        cov = dot(weighted, x_ref[...])
        low = cov[half:, half:]
        tri = jnp.where(row <= col, cov[:half, :half], low)
        diag = jnp.sum(jnp.where(row == col, low, 0.0), axis=0, keepdims=True)
        vec = sums[pl.ds(region, 1), :]
        extra = jnp.where(
            line == 0,
            diag,
            jnp.where(line == 1, vec[:, :half], jnp.where(line == 2, vec[:, half:], 0.0)),
        )
        return cov[:half, half:], tri, extra

    def store(ref, group, parts):
        kind = ref.dtype
        ref[group, 0:half, :] = parts[0].astype(kind)
        ref[group, half:members, :] = parts[1].astype(kind)
        ref[group, members : members + EXTRA, :] = parts[2].astype(kind)

    def copy1(group):
        return pltpu.make_async_remote_copy(
            src_ref=tx1.at[group],
            dst_ref=rx1.at[group],
            send_sem=send1.at[group],
            recv_sem=recv1.at[group],
            device_id=(partner, me_l),
            device_id_type=MESH,
        )

    def copy2(to, slot):
        return pltpu.make_async_remote_copy(
            src_ref=tx2.at[to],
            dst_ref=rx2.at[slot],
            send_sem=send2.at[to],
            recv_sem=recv2.at[slot],
            device_id=(to * 2 + side, me_l),
            device_id_type=MESH,
        )

    def copy3(to, slot):
        return pltpu.make_async_remote_copy(
            src_ref=tx3,
            dst_ref=rx3.at[slot],
            send_sem=send3.at[to],
            recv_sem=recv3.at[slot],
            device_id=(me_r, to),
            device_id_type=MESH,
        )

    store(tx1, other_group(0), contribution(other_group(0) * 2 + (1 - side)))
    pl.semaphore_wait(barrier, 1 + (groups - 1) + (levels - 1))
    copy1(other_group(0)).start()

    def give(k):
        group = other_group(k + 1)
        store(tx1, group, contribution(group * 2 + (1 - side)))
        copy1(group).start()

    each(groups - 1, give)

    def hold(k):
        group = other_group(k)
        store(keep, group, contribution(group * 2 + side))

    each(groups, hold)

    def fold(k):
        group = other_group(k)
        copy1(group).wait_recv()
        tx2[group] = (keep[group] + rx1[group].astype(F32)).astype(BF16)
        copy2(group, my_group).start()

    each(groups - 1, fold)
    copy1(my_group).wait_recv()
    keep[my_group] = keep[my_group] + rx1[my_group].astype(F32)

    def gather(k):
        group = other_group(k)
        copy2(group, group).wait_recv()
        keep[my_group] = keep[my_group] + rx2[group].astype(F32)

    each(groups - 1, gather)
    total = keep[my_group]
    tx3[...] = total.astype(BF16)
    each(levels - 1, lambda k: copy3(other_level(k), me_l).start())
    for k in range(levels - 1):
        level = other_level(k)
        apart = jnp.abs(level - me_l)
        factor = jnp.float32(0.0)
        for distance in range(1, levels):
            factor = jnp.where(apart == distance, jnp.float32(0.5**distance), factor)
        copy3(level, level).wait_recv()
        total = total + factor * rx3[level].astype(F32)

    corner = total[:half]
    tri = total[half:members]
    flip = tri.T
    shift = members - 1.0
    mat[0:half, half:members] = corner
    mat[half:members, 0:half] = corner.T
    mat[0:half, 0:half] = jnp.where(row <= col, tri, flip) + jnp.where(row == col, shift, 0.0)
    mat[half:members, half:members] = jnp.where(
        row == col,
        total[members : members + 1] + shift,
        jnp.where(row > col, tri, flip),
    )
    vector = jnp.concatenate(
        [total[members + 1 : members + 2], total[members + 2 : members + 3]], axis=1
    )
    matrix = mat[...]
    norm = 0.5 * jnp.sqrt(
        jnp.sum(jnp.sum(matrix * matrix, axis=0, keepdims=True), axis=1, keepdims=True)
    )
    eye = (
        lax.broadcasted_iota(jnp.int32, (members, members), 0)
        == lax.broadcasted_iota(jnp.int32, (members, members), 1)
    ).astype(F32)
    middle = jnp.sum(
        jnp.sum(matrix * eye, axis=0, keepdims=True), axis=1, keepdims=True
    ) / (members * norm)
    root_iter = shifted(middle, matrix / norm - middle * eye)
    inverse_iter = correct(root_iter)
    root_iter = product(root_iter, inverse_iter)
    for step in range(1, NSTEPS):
        correction = correct(product(inverse_iter, root_iter))
        if step < NSTEPS - 1:
            root_iter = product(root_iter, correction)
        inverse_iter = product(correction, inverse_iter)
    mean_shift = apply(inverse_iter, apply(inverse_iter, vector)) / norm
    scale = math.sqrt(members - 1.0) * lax.rsqrt(norm)
    table = scale * (inverse_iter[0] * eye + inverse_iter[1]) + mean_shift
    spare = (1.0 - jnp.sum(table, axis=1, keepdims=True)) * (1.0 / members)
    out_ref[...] = (table + spare).astype(BF16)

    each(groups, lambda k: copy1(other_group(k)).wait_send())
    each(groups - 1, lambda k: copy2(other_group(k), my_group).wait_send())
    each(levels - 1, lambda k: copy3(other_level(k), me_l).wait_send())


def body(ensemble, obs_anomaly, innovation, obs_precision, owner_region, neighbours):
    regions = lax.axis_size("region")
    levels = lax.axis_size("level")
    groups = regions // 2
    obs, members = obs_anomaly.shape[1:]
    rows, half = members + EXTRA, members // 2
    vmem = pl.BlockSpec(memory_space=pltpu.VMEM)
    hbm = pl.BlockSpec(memory_space=pltpu.HBM)
    dma = pltpu.SemaphoreType.DMA
    table = pl.pallas_call(
        functools.partial(weights_kernel, regions, levels),
        out_shape=jax.ShapeDtypeStruct((members, members), BF16),
        in_specs=[hbm] * 5,
        out_specs=vmem,
        scratch_shapes=[
            pltpu.VMEM((obs, members), BF16),
            pltpu.VMEM((1, obs), jnp.int32),
            pltpu.VMEM((1, obs), BF16),
            pltpu.VMEM((1, obs), BF16),
            pltpu.VMEM(neighbours.shape[::-1], jnp.int32),
            dma((5,)),
            pltpu.VMEM((regions, obs), F32),
            pltpu.VMEM((regions, members), F32),
            pltpu.VMEM((members, obs), F32),
            pltpu.VMEM((groups, rows, half), BF16),
            pltpu.VMEM((groups, rows, half), F32),
            pltpu.VMEM((groups, rows, half), BF16),
            pltpu.VMEM((groups, rows, half), BF16),
            pltpu.VMEM((groups, rows, half), BF16),
            pltpu.VMEM((rows, half), BF16),
            pltpu.VMEM((levels, rows, half), BF16),
            pltpu.VMEM((members, members), F32),
            dma((groups,)),
            dma((groups,)),
            dma((groups,)),
            dma((groups,)),
            dma((levels,)),
            dma((levels,)),
        ],
        compiler_params=pltpu.CompilerParams(
            collective_id=0, has_side_effects=True, vmem_limit_bytes=61 * 2**20
        ),
    )(
        obs_anomaly[0],
        owner_region.reshape(1, obs),
        obs_precision,
        innovation,
        neighbours.T,
    )
    return dot(table, ensemble[0]).astype(BF16)[None]


def solution(mesh):
    return jax.shard_map(
        body,
        mesh=mesh,
        in_specs=(
            P("level", None, "region"),
            P("level", "region", None),
            P("level", "region"),
            P("level", "region"),
            P("level", "region", None),
            P(),
        ),
        out_specs=P("level", None, "region"),
        check_vma=False,
    )
```

```python
import functools
import math

import jax
import jax.numpy as jnp
from jax import lax
from jax.experimental import pallas as pl
from jax.experimental.pallas import tpu as pltpu
from jax.sharding import PartitionSpec as P

NSTEPS = 4
TAPER = 0.6
EXTRA = 16
F32 = jnp.float32
BF16 = jnp.bfloat16
MESH = pl.DeviceIdType.MESH


def each(count, step):
    if count <= 8:
        for k in range(count):
            step(k)
    else:
        lax.fori_loop(0, count, lambda k, c: (step(k), c)[1], 0)


def dot(a, b):
    return jnp.dot(a, b, preferred_element_type=F32)


def shifted(scale, rest):
    return scale, rest, rest.astype(BF16)


def product(a, b):
    return shifted(a[0] * b[0], a[0] * b[1] + b[0] * a[1] + dot(a[2], b[2]))


def correct(a):
    return shifted(1.5 - 0.5 * a[0], -0.5 * a[1])


def apply(a, vector):
    rows = jnp.broadcast_to(vector, (8, vector.shape[1]))
    high = rows.astype(BF16)
    low = (rows - high.astype(F32)).astype(BF16)
    return (a[0] * rows + (dot(high, a[2]) + dot(low, a[2])))[0:1]


def weights_kernel(
    regions,
    levels,
    x_hbm,
    owner_hbm,
    prec_hbm,
    innov_hbm,
    neigh_hbm,
    out_ref,
    x_ref,
    owner_ref,
    prec_ref,
    innov_ref,
    neigh_ref,
    load_sem,
    gain,
    sums,
    xt,
    tx1,
    keep,
    rx1,
    tx2,
    rx2,
    tx3,
    rx3,
    mat,
    send1,
    recv1,
    send2,
    recv2,
    send3,
    recv3,
):
    groups = regions // 2
    members = x_ref.shape[1]
    half = members // 2
    me_r = lax.axis_index("region")
    me_l = lax.axis_index("level")
    my_group, side = lax.div(me_r, 2), lax.rem(me_r, 2)
    partner = my_group * 2 + (1 - side)

    def other_group(k):
        return lax.rem(my_group + 1 + k, groups)

    def other_level(k):
        return lax.rem(me_l + 1 + k, levels)

    loads = [
        pltpu.make_async_copy(source, target, load_sem.at[n])
        for n, (source, target) in enumerate(
            (
                (neigh_hbm, neigh_ref),
                (owner_hbm, owner_ref),
                (prec_hbm, prec_ref),
                (innov_hbm, innov_ref),
                (x_hbm, x_ref),
            )
        )
    ]
    for load in loads:
        load.start()

    barrier = pltpu.get_barrier_semaphore()

    def greet(region, level):
        pl.semaphore_signal(barrier, inc=1, device_id=(region, level), device_id_type=MESH)

    greet(partner, me_l)
    each(groups - 1, lambda k: greet(other_group(k) * 2 + side, me_l))
    each(levels - 1, lambda k: greet(me_r, other_level(k)))

    for load in loads[:4]:
        load.wait()
    owner = owner_ref[...]
    unit = (
        lax.broadcasted_iota(jnp.int32, (regions, regions), 0)
        == lax.broadcasted_iota(jnp.int32, (regions, regions), 1)
    ).astype(F32)
    lists = lax.dot_general(
        unit.astype(BF16),
        neigh_ref[...].astype(F32).astype(BF16),
        (((1,), (1,)), ((), ())),
        preferred_element_type=F32,
    ).astype(jnp.int32)
    ids = lax.broadcasted_iota(jnp.int32, (regions, owner.shape[1]), 0)
    weight = (ids == owner).astype(F32)
    for listed in range(neigh_ref.shape[0]):
        hit = (lists[:, listed : listed + 1] == owner).astype(F32)
        weight = weight + TAPER ** (listed + 1) * hit
    rounded = (weight * prec_ref[...].astype(F32)).astype(BF16).astype(F32)
    gain[...] = rounded
    loads[4].wait()
    sums[...] = dot((rounded * innov_ref[...].astype(F32)).astype(BF16), x_ref[...])
    xt[...] = x_ref[...].astype(F32).T

    row = lax.broadcasted_iota(jnp.int32, (half, half), 0)
    col = lax.broadcasted_iota(jnp.int32, (half, half), 1)
    line = lax.broadcasted_iota(jnp.int32, (EXTRA, half), 0)

    def contribution(region):
        weighted = (xt[...] * gain[pl.ds(region, 1), :]).astype(BF16)
        cov = dot(weighted, x_ref[...])
        low = cov[half:, half:]
        tri = jnp.where(row <= col, cov[:half, :half], low)
        diag = jnp.sum(jnp.where(row == col, low, 0.0), axis=0, keepdims=True)
        vec = sums[pl.ds(region, 1), :]
        extra = jnp.where(
            line == 0,
            diag,
            jnp.where(line == 1, vec[:, :half], jnp.where(line == 2, vec[:, half:], 0.0)),
        )
        return cov[:half, half:], tri, extra

    def store(ref, group, parts):
        kind = ref.dtype
        ref[group, 0:half, :] = parts[0].astype(kind)
        ref[group, half:members, :] = parts[1].astype(kind)
        ref[group, members : members + EXTRA, :] = parts[2].astype(kind)

    spans = (pl.ds(0, half), pl.ds(half, half + EXTRA))

    def copy1(group, part):
        return pltpu.make_async_remote_copy(
            src_ref=tx1.at[group, spans[part]],
            dst_ref=rx1.at[group, spans[part]],
            send_sem=send1.at[part, group],
            recv_sem=recv1.at[part, group],
            device_id=(partner, me_l),
            device_id_type=MESH,
        )

    def copy2(to, slot, part):
        return pltpu.make_async_remote_copy(
            src_ref=tx2.at[to, spans[part]],
            dst_ref=rx2.at[slot, spans[part]],
            send_sem=send2.at[part, to],
            recv_sem=recv2.at[part, slot],
            device_id=(to * 2 + side, me_l),
            device_id_type=MESH,
        )

    def copy3(to, slot, part):
        return pltpu.make_async_remote_copy(
            src_ref=tx3.at[spans[part]],
            dst_ref=rx3.at[slot, spans[part]],
            send_sem=send3.at[part, to],
            recv_sem=recv3.at[part, slot],
            device_id=(me_r, to),
            device_id_type=MESH,
        )

    def hold(group):
        store(keep, group, contribution(group * 2 + side))

    def fold(k, part):
        group, span = other_group(k), spans[part]
        copy1(group, part).wait_recv()
        tx2[group, span] = (keep[group, span] + rx1[group, span].astype(F32)).astype(BF16)
        copy2(group, my_group, part).start()

    def gather(part):
        span = spans[part]
        copy1(my_group, part).wait_recv()
        keep[my_group, span] = keep[my_group, span] + rx1[my_group, span].astype(F32)

        def add(k):
            group = other_group(k)
            copy2(group, group, part).wait_recv()
            keep[my_group, span] = keep[my_group, span] + rx2[group, span].astype(F32)

        each(groups - 1, add)
        tx3[span] = keep[my_group, span].astype(BF16)
        each(levels - 1, lambda k: copy3(other_level(k), me_l, part).start())

    def mix(part):
        total = keep[my_group, spans[part]]
        for k in range(levels - 1):
            level = other_level(k)
            apart = jnp.abs(level - me_l)
            factor = jnp.float32(0.0)
            for distance in range(1, levels):
                factor = jnp.where(apart == distance, jnp.float32(0.5**distance), factor)
            copy3(level, level, part).wait_recv()
            total = total + factor * rx3[level, spans[part]].astype(F32)
        return total

    store(tx1, other_group(0), contribution(other_group(0) * 2 + (1 - side)))
    pl.semaphore_wait(barrier, 1 + (groups - 1) + (levels - 1))
    copy1(other_group(0), 0).start()

    def give(k):
        group = other_group(k + 1)
        store(tx1, group, contribution(group * 2 + (1 - side)))
        copy1(group, 0).start()

    each(groups - 1, give)
    each(groups, lambda k: copy1(other_group(k), 1).start())

    def hold_fold(k):
        hold(other_group(k))
        fold(k, 0)

    each(groups - 1, hold_fold)
    hold(my_group)
    ahead = (groups - 1) * 2 // 3
    each(ahead, lambda k: fold(k, 1))
    gather(0)
    each(groups - 1 - ahead, lambda k: fold(k + ahead, 1))
    gather(1)

    corner = mix(0)
    shift = members - 1.0
    mat[0:half, half:members] = corner
    mat[half:members, 0:half] = corner.T
    total = mix(1)
    tri = total[:half]
    flip = tri.T
    mat[0:half, 0:half] = jnp.where(row <= col, tri, flip) + jnp.where(row == col, shift, 0.0)
    mat[half:members, half:members] = jnp.where(
        row == col,
        total[half : half + 1] + shift,
        jnp.where(row > col, tri, flip),
    )
    vector = jnp.concatenate(
        [total[half + 1 : half + 2], total[half + 2 : half + 3]], axis=1
    )
    matrix = mat[...]
    norm = 0.5 * jnp.sqrt(
        jnp.sum(jnp.sum(matrix * matrix, axis=0, keepdims=True), axis=1, keepdims=True)
    )
    eye = (
        lax.broadcasted_iota(jnp.int32, (members, members), 0)
        == lax.broadcasted_iota(jnp.int32, (members, members), 1)
    ).astype(F32)
    middle = jnp.sum(
        jnp.sum(matrix * eye, axis=0, keepdims=True), axis=1, keepdims=True
    ) / (members * norm)
    root_iter = shifted(middle, matrix / norm - middle * eye)
    inverse_iter = correct(root_iter)
    root_iter = product(root_iter, inverse_iter)
    for step in range(1, NSTEPS):
        if step == NSTEPS - 1:
            vector = apply(inverse_iter, apply(inverse_iter, vector))
        correction = correct(product(inverse_iter, root_iter))
        if step < NSTEPS - 1:
            root_iter = product(root_iter, correction)
        inverse_iter = product(correction, inverse_iter)
    mean_shift = apply(correction, apply(correction, vector)) / norm
    scale = math.sqrt(members - 1.0) * lax.rsqrt(norm)
    table = scale * (inverse_iter[0] * eye + inverse_iter[1]) + mean_shift
    spare = (1.0 - jnp.sum(table, axis=1, keepdims=True)) * (1.0 / members)
    out_ref[...] = (table + spare).astype(BF16)

    for part in range(2):
        each(groups, lambda k: copy1(other_group(k), part).wait_send())
        each(groups - 1, lambda k: copy2(other_group(k), my_group, part).wait_send())
        each(levels - 1, lambda k: copy3(other_level(k), me_l, part).wait_send())


def update_kernel(pieces, table_hbm, block_ref, out_hbm, table, held, load_sem, store_sem):
    load = pltpu.make_async_copy(table_hbm, table, load_sem)
    load.start()
    load.wait()
    width = block_ref.shape[2] // pieces
    stores = []
    for n in range(pieces):
        columns = pl.ds(n * width, width)
        held[:, columns] = dot(table[...], block_ref[0, :, columns]).astype(BF16)
        stores.append(
            pltpu.make_async_copy(held.at[:, columns], out_hbm.at[0, :, columns], store_sem.at[n])
        )
        stores[n].start()
    for store in stores:
        store.wait()


def body(ensemble, obs_anomaly, innovation, obs_precision, owner_region, neighbours):
    regions = lax.axis_size("region")
    levels = lax.axis_size("level")
    groups = regions // 2
    obs, members = obs_anomaly.shape[1:]
    rows, half = members + EXTRA, members // 2
    vmem = pl.BlockSpec(memory_space=pltpu.VMEM)
    hbm = pl.BlockSpec(memory_space=pltpu.HBM)
    dma = pltpu.SemaphoreType.DMA
    table = pl.pallas_call(
        functools.partial(weights_kernel, regions, levels),
        out_shape=jax.ShapeDtypeStruct((members, members), BF16),
        in_specs=[hbm] * 5,
        out_specs=vmem,
        scratch_shapes=[
            pltpu.VMEM((obs, members), BF16),
            pltpu.VMEM((1, obs), jnp.int32),
            pltpu.VMEM((1, obs), BF16),
            pltpu.VMEM((1, obs), BF16),
            pltpu.VMEM(neighbours.shape[::-1], jnp.int32),
            dma((5,)),
            pltpu.VMEM((regions, obs), F32),
            pltpu.VMEM((regions, members), F32),
            pltpu.VMEM((members, obs), F32),
            pltpu.VMEM((groups, rows, half), BF16),
            pltpu.VMEM((groups, rows, half), F32),
            pltpu.VMEM((groups, rows, half), BF16),
            pltpu.VMEM((groups, rows, half), BF16),
            pltpu.VMEM((groups, rows, half), BF16),
            pltpu.VMEM((rows, half), BF16),
            pltpu.VMEM((levels, rows, half), BF16),
            pltpu.VMEM((members, members), F32),
            dma((2, groups)),
            dma((2, groups)),
            dma((2, groups)),
            dma((2, groups)),
            dma((2, levels)),
            dma((2, levels)),
        ],
        compiler_params=pltpu.CompilerParams(
            collective_id=0, has_side_effects=True, vmem_limit_bytes=61 * 2**20
        ),
        cost_estimate=pl.CostEstimate(
            flops=20 * obs * members * members * regions,
            bytes_accessed=64 * obs * members,
            transcendentals=0,
        ),
    )(
        obs_anomaly[0],
        owner_region.reshape(1, obs),
        obs_precision,
        innovation,
        neighbours.T,
    )
    pieces = 8
    return pl.pallas_call(
        functools.partial(update_kernel, pieces),
        out_shape=jax.ShapeDtypeStruct(ensemble.shape, BF16),
        in_specs=[hbm, vmem],
        out_specs=hbm,
        scratch_shapes=[
            pltpu.VMEM((members, members), BF16),
            pltpu.VMEM(ensemble.shape[1:], BF16),
            dma(()),
            dma((pieces,)),
        ],
        compiler_params=pltpu.CompilerParams(vmem_limit_bytes=16 * 2**20),
    )(table, ensemble)


def solution(mesh):
    return jax.shard_map(
        body,
        mesh=mesh,
        in_specs=(
            P("level", None, "region"),
            P("level", "region", None),
            P("level", "region"),
            P("level", "region"),
            P("level", "region", None),
            P(),
        ),
        out_specs=P("level", None, "region"),
        check_vma=False,
    )
```

```python
import functools
import math

import jax
import jax.numpy as jnp
from jax import lax
from jax.experimental import pallas as pl
from jax.experimental.pallas import tpu as pltpu
from jax.sharding import PartitionSpec as P

NSTEPS = 4
TAPER = 0.6
EXTRA = 16
F32 = jnp.float32
BF16 = jnp.bfloat16
MESH = pl.DeviceIdType.MESH


def each(count, step):
    if count <= 8:
        for k in range(count):
            step(k)
    else:
        lax.fori_loop(0, count, lambda k, c: (step(k), c)[1], 0)


def dot(a, b):
    return jnp.dot(a, b, preferred_element_type=F32)


def shifted(scale, rest):
    return scale, rest, rest.astype(BF16)


def product(a, b):
    return shifted(a[0] * b[0], a[0] * b[1] + b[0] * a[1] + dot(a[2], b[2]))


def correct(a):
    return shifted(1.5 - 0.5 * a[0], -0.5 * a[1])


def apply(a, vector):
    rows = jnp.broadcast_to(vector, (8, vector.shape[1]))
    high = rows.astype(BF16)
    low = (rows - high.astype(F32)).astype(BF16)
    return (a[0] * rows + (dot(high, a[2]) + dot(low, a[2])))[0:1]


def weights_kernel(
    regions,
    levels,
    x_hbm,
    owner_hbm,
    prec_hbm,
    innov_hbm,
    neigh_hbm,
    out_ref,
    x_ref,
    owner_ref,
    prec_ref,
    innov_ref,
    neigh_ref,
    load_sem,
    gain,
    sums,
    xt,
    tx1,
    keep,
    rx1,
    tx2,
    rx2,
    tx3,
    rx3,
    mat,
    send1,
    recv1,
    send2,
    recv2,
    send3,
    recv3,
):
    groups = regions // 2
    members = x_ref.shape[1]
    half = members // 2
    me_r = lax.axis_index("region")
    me_l = lax.axis_index("level")
    my_group, side = lax.div(me_r, 2), lax.rem(me_r, 2)
    partner = my_group * 2 + (1 - side)

    def other_group(k):
        return lax.rem(my_group + 1 + k, groups)

    def other_level(k):
        return lax.rem(me_l + 1 + k, levels)

    loads = [
        pltpu.make_async_copy(source, target, load_sem.at[n])
        for n, (source, target) in enumerate(
            (
                (x_hbm, x_ref),
                (neigh_hbm, neigh_ref),
                (owner_hbm, owner_ref),
                (prec_hbm, prec_ref),
                (innov_hbm, innov_ref),
            )
        )
    ]
    for load in loads:
        load.start()

    barrier = pltpu.get_barrier_semaphore()

    def greet(region, level):
        pl.semaphore_signal(barrier, inc=1, device_id=(region, level), device_id_type=MESH)

    greet(partner, me_l)
    each(groups - 1, lambda k: greet(other_group(k) * 2 + side, me_l))
    each(levels - 1, lambda k: greet(me_r, other_level(k)))

    for load in loads[1:]:
        load.wait()
    owner = owner_ref[...]
    unit = (
        lax.broadcasted_iota(jnp.int32, (regions, regions), 0)
        == lax.broadcasted_iota(jnp.int32, (regions, regions), 1)
    ).astype(F32)
    lists = lax.dot_general(
        unit.astype(BF16),
        neigh_ref[...].astype(F32).astype(BF16),
        (((1,), (1,)), ((), ())),
        preferred_element_type=F32,
    ).astype(jnp.int32)
    ids = lax.broadcasted_iota(jnp.int32, (regions, owner.shape[1]), 0)
    weight = (ids == owner).astype(F32)
    for listed in range(neigh_ref.shape[0]):
        hit = (lists[:, listed : listed + 1] == owner).astype(F32)
        weight = weight + TAPER ** (listed + 1) * hit
    rounded = (weight * prec_ref[...].astype(F32)).astype(BF16).astype(F32)
    gain[...] = rounded
    loads[0].wait()
    sums[...] = dot((rounded * innov_ref[...].astype(F32)).astype(BF16), x_ref[...])
    xt[...] = x_ref[...].T

    row = lax.broadcasted_iota(jnp.int32, (half, half), 0)
    col = lax.broadcasted_iota(jnp.int32, (half, half), 1)
    line = lax.broadcasted_iota(jnp.int32, (EXTRA, half), 0)

    def contribution(region):
        weighted = xt[...] * gain[pl.ds(region, 1), :].astype(BF16)
        cov = dot(weighted, x_ref[...])
        low = cov[half:, half:]
        tri = jnp.where(row <= col, cov[:half, :half], low)
        diag = jnp.sum(jnp.where(row == col, low, 0.0), axis=0, keepdims=True)
        vec = sums[pl.ds(region, 1), :]
        extra = jnp.where(
            line == 0,
            diag,
            jnp.where(line == 1, vec[:, :half], jnp.where(line == 2, vec[:, half:], 0.0)),
        )
        return cov[:half, half:], tri, extra

    def store(ref, group, parts):
        kind = ref.dtype
        ref[group, 0:half, :] = parts[0].astype(kind)
        ref[group, half:members, :] = parts[1].astype(kind)
        ref[group, members : members + EXTRA, :] = parts[2].astype(kind)

    spans = (pl.ds(0, half), pl.ds(half, half + EXTRA))

    def copy1(group, part):
        return pltpu.make_async_remote_copy(
            src_ref=tx1.at[group, spans[part]],
            dst_ref=rx1.at[group, spans[part]],
            send_sem=send1.at[part, group],
            recv_sem=recv1.at[part, group],
            device_id=(partner, me_l),
            device_id_type=MESH,
        )

    def copy2(to, slot, part):
        return pltpu.make_async_remote_copy(
            src_ref=tx2.at[to, spans[part]],
            dst_ref=rx2.at[slot, spans[part]],
            send_sem=send2.at[part, to],
            recv_sem=recv2.at[part, slot],
            device_id=(to * 2 + side, me_l),
            device_id_type=MESH,
        )

    def copy3(to, slot, part):
        return pltpu.make_async_remote_copy(
            src_ref=tx3.at[spans[part]],
            dst_ref=rx3.at[slot, spans[part]],
            send_sem=send3.at[part, to],
            recv_sem=recv3.at[part, slot],
            device_id=(me_r, to),
            device_id_type=MESH,
        )

    def hold(group):
        store(keep, group, contribution(group * 2 + side))

    def fold(k, part):
        group, span = other_group(k), spans[part]
        copy1(group, part).wait_recv()
        tx2[group, span] = (keep[group, span] + rx1[group, span].astype(F32)).astype(BF16)
        copy2(group, my_group, part).start()

    def gather(part):
        span = spans[part]
        copy1(my_group, part).wait_recv()
        keep[my_group, span] = keep[my_group, span] + rx1[my_group, span].astype(F32)

        def add(k):
            group = other_group(k)
            copy2(group, group, part).wait_recv()
            keep[my_group, span] = keep[my_group, span] + rx2[group, span].astype(F32)

        each(groups - 1, add)
        tx3[span] = keep[my_group, span].astype(BF16)
        each(levels - 1, lambda k: copy3(other_level(k), me_l, part).start())

    def mix(part):
        total = keep[my_group, spans[part]]
        for k in range(levels - 1):
            level = other_level(k)
            apart = jnp.abs(level - me_l)
            factor = jnp.float32(0.0)
            for distance in range(1, levels):
                factor = jnp.where(apart == distance, jnp.float32(0.5**distance), factor)
            copy3(level, level, part).wait_recv()
            total = total + factor * rx3[level, spans[part]].astype(F32)
        return total

    store(tx1, other_group(0), contribution(other_group(0) * 2 + (1 - side)))
    pl.semaphore_wait(barrier, 1 + (groups - 1) + (levels - 1))
    copy1(other_group(0), 0).start()

    def give(k):
        group = other_group(k + 1)
        store(tx1, group, contribution(group * 2 + (1 - side)))
        copy1(group, 0).start()

    each(groups - 1, give)
    each(groups, lambda k: copy1(other_group(k), 1).start())

    def hold_fold(k):
        hold(other_group(k))
        fold(k, 0)

    each(groups - 1, hold_fold)
    hold(my_group)
    ahead = (groups - 1) * 2 // 3
    each(ahead, lambda k: fold(k, 1))
    gather(0)
    each(groups - 1 - ahead, lambda k: fold(k + ahead, 1))
    gather(1)

    corner = mix(0)
    shift = members - 1.0
    mat[0:half, half:members] = corner
    mat[half:members, 0:half] = corner.T
    total = mix(1)
    tri = total[:half]
    flip = tri.T
    mat[0:half, 0:half] = jnp.where(row <= col, tri, flip) + jnp.where(row == col, shift, 0.0)
    mat[half:members, half:members] = jnp.where(
        row == col,
        total[half : half + 1] + shift,
        jnp.where(row > col, tri, flip),
    )
    vector = jnp.concatenate(
        [total[half + 1 : half + 2], total[half + 2 : half + 3]], axis=1
    )
    matrix = mat[...]
    norm = 0.5 * jnp.sqrt(
        jnp.sum(jnp.sum(matrix * matrix, axis=0, keepdims=True), axis=1, keepdims=True)
    )
    eye = (
        lax.broadcasted_iota(jnp.int32, (members, members), 0)
        == lax.broadcasted_iota(jnp.int32, (members, members), 1)
    ).astype(F32)
    middle = jnp.sum(
        jnp.sum(matrix * eye, axis=0, keepdims=True), axis=1, keepdims=True
    ) / (members * norm)
    root_iter = shifted(middle, matrix / norm - middle * eye)
    inverse_iter = correct(root_iter)
    root_iter = product(root_iter, inverse_iter)
    for step in range(1, NSTEPS):
        if step == NSTEPS - 1:
            vector = apply(inverse_iter, apply(inverse_iter, vector))
        correction = correct(product(inverse_iter, root_iter))
        if step < NSTEPS - 1:
            root_iter = product(root_iter, correction)
        inverse_iter = product(correction, inverse_iter)
    mean_shift = apply(correction, apply(correction, vector)) / norm
    scale = math.sqrt(members - 1.0) * lax.rsqrt(norm)
    table = scale * (inverse_iter[0] * eye + inverse_iter[1]) + mean_shift
    spare = (1.0 - jnp.sum(table, axis=1, keepdims=True)) * (1.0 / members)
    out_ref[...] = (table + spare).astype(BF16)

    for part in range(2):
        each(groups, lambda k: copy1(other_group(k), part).wait_send())
        each(groups - 1, lambda k: copy2(other_group(k), my_group, part).wait_send())
        each(levels - 1, lambda k: copy3(other_level(k), me_l, part).wait_send())


def update_kernel(
    pieces, table_hbm, block_hbm, out_hbm, table, block, held, table_sem, load_sem, store_sem
):
    width = block.shape[1] // pieces
    first = pltpu.make_async_copy(table_hbm, table, table_sem)
    first.start()
    loads = []
    for n in range(pieces):
        columns = pl.ds(n * width, width)
        loads.append(
            pltpu.make_async_copy(block_hbm.at[0, :, columns], block.at[:, columns], load_sem.at[n])
        )
        loads[n].start()
    first.wait()
    stores = []
    for n in range(pieces):
        columns = pl.ds(n * width, width)
        loads[n].wait()
        held[:, columns] = dot(table[...], block[:, columns]).astype(BF16)
        stores.append(
            pltpu.make_async_copy(held.at[:, columns], out_hbm.at[0, :, columns], store_sem.at[n])
        )
        stores[n].start()
    for store in stores:
        store.wait()


def body(ensemble, obs_anomaly, innovation, obs_precision, owner_region, neighbours):
    regions = lax.axis_size("region")
    levels = lax.axis_size("level")
    groups = regions // 2
    obs, members = obs_anomaly.shape[1:]
    rows, half = members + EXTRA, members // 2
    vmem = pl.BlockSpec(memory_space=pltpu.VMEM)
    hbm = pl.BlockSpec(memory_space=pltpu.HBM)
    dma = pltpu.SemaphoreType.DMA
    table = pl.pallas_call(
        functools.partial(weights_kernel, regions, levels),
        out_shape=jax.ShapeDtypeStruct((members, members), BF16),
        in_specs=[hbm] * 5,
        out_specs=vmem,
        scratch_shapes=[
            pltpu.VMEM((obs, members), BF16),
            pltpu.VMEM((1, obs), jnp.int32),
            pltpu.VMEM((1, obs), BF16),
            pltpu.VMEM((1, obs), BF16),
            pltpu.VMEM(neighbours.shape[::-1], jnp.int32),
            dma((5,)),
            pltpu.VMEM((regions, obs), F32),
            pltpu.VMEM((regions, members), F32),
            pltpu.VMEM((members, obs), BF16),
            pltpu.VMEM((groups, rows, half), BF16),
            pltpu.VMEM((groups, rows, half), F32),
            pltpu.VMEM((groups, rows, half), BF16),
            pltpu.VMEM((groups, rows, half), BF16),
            pltpu.VMEM((groups, rows, half), BF16),
            pltpu.VMEM((rows, half), BF16),
            pltpu.VMEM((levels, rows, half), BF16),
            pltpu.VMEM((members, members), F32),
            dma((2, groups)),
            dma((2, groups)),
            dma((2, groups)),
            dma((2, groups)),
            dma((2, levels)),
            dma((2, levels)),
        ],
        compiler_params=pltpu.CompilerParams(
            collective_id=0, has_side_effects=True, vmem_limit_bytes=61 * 2**20
        ),
        cost_estimate=pl.CostEstimate(
            flops=20 * obs * members * members * regions,
            bytes_accessed=64 * obs * members,
            transcendentals=0,
        ),
    )(
        obs_anomaly[0],
        owner_region.reshape(1, obs),
        obs_precision,
        innovation,
        neighbours.T,
    )
    pieces = 8
    return pl.pallas_call(
        functools.partial(update_kernel, pieces),
        out_shape=jax.ShapeDtypeStruct(ensemble.shape, BF16),
        in_specs=[hbm, hbm],
        out_specs=hbm,
        scratch_shapes=[
            pltpu.VMEM((members, members), BF16),
            pltpu.VMEM(ensemble.shape[1:], BF16),
            pltpu.VMEM(ensemble.shape[1:], BF16),
            dma(()),
            dma((pieces,)),
            dma((pieces,)),
        ],
        compiler_params=pltpu.CompilerParams(vmem_limit_bytes=61 * 2**20),
    )(table, ensemble)


def solution(mesh):
    return jax.shard_map(
        body,
        mesh=mesh,
        in_specs=(
            P("level", None, "region"),
            P("level", "region", None),
            P("level", "region"),
            P("level", "region"),
            P("level", "region", None),
            P(),
        ),
        out_specs=P("level", None, "region"),
        check_vma=False,
    )
```
